512 devices in a mesh: seq: 64 (over x, z_hi, y), ch: 8 (over z_lo, core).
Axes of the slice: x: 4, y: 8, z: 8 (z_hi: 2, z_lo: 4; z = z_hi * 4 + z_lo), core: 2. Of those that a mesh axis runs over, the one named last changes fastest.
Arguments:
- gate_input: bfloat16 [16384, 4096], P('seq', 'ch'), may hold values from -6 to 6
- key_input: bfloat16 [16384, 4096], P('seq', 'ch'), may hold values from -6 to 6
- value_input: bfloat16 [16384, 4096], P('seq', 'ch'), may hold values from -6 to 6
- decay_rate: float32 [4096, 16], P('ch'), as said below
- residues: float32 [4096, 16], P('ch'), may hold values from -1.5 to 1.5
- out_weight: bfloat16 [4096, 4096], P('ch', 'seq'), may hold values from -0.09375 to 0.09375
Outputs:
- mixed: bfloat16 [16384, 4096], P(('seq', 'ch'))
The draws below stay inside these ranges and needn't reach their ends.
Inputs may be any that keep to these rules, and one draw needn't show every extreme that they name: `decay_rate`: every entry is positive and at most 0.05.
All inputs are finite; a program needn't handle non-finite values.
Results may differ from the reference program's by a relative error of at most 0.025.
Values may be sent and summed in bfloat16 or wider, within the bound.
No kernel may reach another device: no remote copies, remote signals or barrier semaphores. Data moves between devices by JAX's collectives and lax.ppermute only.
A program may use at most 64 MiB of HBM per device.

```python
import math
import jax
import jax.numpy as jnp
from jax import lax

CHANNELS = 4096
OUTPUTS = 4096
POLES = 16
TOKENS = 16384
N_CH = 8


def draw_decay_rate(key, part):
    key = jax.random.fold_in(key, 11)
    first_key, second_key = jax.random.split(key)
    share = 0.4
    quick = jax.random.uniform(first_key, (CHANNELS, 1), jnp.float32) < share
    spread = jax.random.uniform(second_key, (CHANNELS, POLES), jnp.float32)
    slow_low = math.log(0.5 / TOKENS)
    middle = math.log(1.0 / 50.0)
    quick_high = math.log(1.0 / 20.0)
    lower = jnp.where(quick, middle, slow_low)
    upper = jnp.where(quick, quick_high, middle)
    return jnp.exp(lower + spread * (upper - lower)).astype(jnp.float32)


def block_levels(key, shape, pieces, low, high):
    factor_of, own = 1.0, jax.random.fold_in(key, 6)
    for axis_at, parts in pieces:
        heights = jnp.exp(jax.random.uniform(jax.random.fold_in(own, axis_at), (parts,), jnp.float32, low / len(pieces), high / len(pieces)))
        factor_of = factor_of * jnp.repeat(heights, shape[axis_at] // parts).reshape([-1 if axis == axis_at else 1 for axis in range(len(shape))])
    return factor_of


def centred(rng, extent, width, most, cuts=(), held_as=jnp.bfloat16):
    result = jax.random.normal(rng, extent, jnp.float32) * width
    if len(cuts) > 0:
        result = block_levels(rng, extent, cuts, -0.22, 0.18) * result
    return jnp.clip(result, min=-most, max=most).astype(held_as)


def setup_inputs(seed: int = 0) -> dict:
    splits = jax.random.split(jax.random.key(seed), 7)
    gate_input = centred(splits[0], (TOKENS, CHANNELS), 1.0, 6.0, ((0, 64), (1, 8)))
    key_input = centred(splits[1], (TOKENS, CHANNELS), 1.0, 6.0, ((0, 64), (1, 8)))
    value_input = centred(splits[2], (TOKENS, CHANNELS), 1.0, 6.0, ((0, 64), (1, 8)))
    decay_rate = draw_decay_rate(jax.random.fold_in(splits[6], 71), 0)
    residues = centred(splits[4], (CHANNELS, POLES), POLES ** -0.5, 1.5, ((0, 8),), jnp.float32)
    out_weight = centred(splits[5], (CHANNELS, OUTPUTS), CHANNELS ** -0.5, 0.09375, ((0, 8), (1, 64)))
    return dict(gate_input=gate_input, key_input=key_input, value_input=value_input, decay_rate=decay_rate, residues=residues, out_weight=out_weight)


def reference(gate_input, key_input, value_input, decay_rate, residues, out_weight):
    signal = key_input.astype(jnp.float32) * value_input.astype(jnp.float32)
    places = jnp.arange(TOKENS).astype(jnp.float32)[:, None]
    impulse = jnp.zeros((TOKENS, CHANNELS), jnp.float32)
    for pole_idx in range(POLES):
        rate = decay_rate[:, pole_idx][None, :]
        amplitude = (residues[:, pole_idx] * jnp.sqrt(decay_rate[:, pole_idx]))[None, :]
        impulse = impulse + amplitude * jnp.exp(-rate * places)
    full_len = 2 * TOKENS
    product = jnp.fft.rfft(signal, n=full_len, axis=0) * jnp.fft.rfft(impulse, n=full_len, axis=0)
    conv = jnp.fft.irfft(product, n=full_len, axis=0)[:TOKENS].astype(jnp.float32)
    gated = (gate_input.astype(jnp.float32) * conv).astype(jnp.bfloat16)
    group_width = CHANNELS // N_CH
    total = jnp.zeros((TOKENS, OUTPUTS), jnp.float32)
    for group in range(N_CH):
        lower = group * group_width
        partial_sum = jnp.dot(gated[:, lower:lower + group_width], out_weight[lower:lower + group_width], preferred_element_type=jnp.float32)
        rounded = lax.optimization_barrier(partial_sum.astype(jnp.bfloat16))
        total = total + rounded.astype(jnp.float32)
    return total.astype(jnp.bfloat16)
```

```python
import jax
import jax.numpy as jnp
from jax import lax
from jax.experimental import pallas as pl
from jax.experimental.pallas import tpu as pltpu
from jax.sharding import Mesh, PartitionSpec as P

AXES = (("x", 4), ("h", 2), ("y", 8), ("z", 4), ("c", 2))
NX, NH, NY, NZ, NC = (size for _, size in AXES)
SEQ = ("x", "h", "y")
CH = ("z", "c")

SUB = 8
LANES = 128
f32 = jnp.float32
bf16 = jnp.bfloat16


def fill_signal(key_ref, value_ref, signal):
    for tile in range(signal.shape[0]):
        lanes = pl.ds(tile * LANES, LANES)
        signal[tile] = key_ref[:, lanes].astype(f32) * value_ref[:, lanes].astype(f32)


def run_states_kernel(key_ref, value_ref, rate_ref, runs_ref, block_ref, signal):
    poles, chans = rate_ref.shape
    steps = key_ref.shape[0] // SUB
    fill_signal(key_ref, value_ref, signal)
    later = (SUB - 1 - lax.broadcasted_iota(jnp.int32, (SUB, LANES), 0)).astype(f32) * steps
    for tile in range(chans // LANES):
        lanes = pl.ds(tile * LANES, LANES)
        rates = [jnp.broadcast_to(rate_ref[pl.ds(r, 1), lanes], (SUB, LANES)) for r in range(poles)]
        decays = [jnp.exp(-rate) for rate in rates]

        def step(j, states):
            x = signal[tile, pl.ds(j, SUB, stride=steps), :]
            return tuple(d * s + x for d, s in zip(decays, states))

        states = lax.fori_loop(0, steps, step, (jnp.zeros((SUB, LANES), f32),) * poles, unroll=4)
        for r in range(poles):
            runs_ref[r, :, lanes] = states[r]
            block_ref[pl.ds(r, 1), lanes] = jnp.sum(
                states[r] * jnp.exp(-rates[r] * later), axis=0, keepdims=True
            )


def run_states(key_input, value_input, rate):
    poles, chans = rate.shape
    return pl.pallas_call(
        run_states_kernel,
        out_shape=(
            jax.ShapeDtypeStruct((poles, SUB, chans), f32),
            jax.ShapeDtypeStruct((poles, chans), f32),
        ),
        scratch_shapes=[pltpu.VMEM((chans // LANES, key_input.shape[0], LANES), f32)],
        compiler_params=pltpu.CompilerParams(vmem_limit_bytes=32 << 20),
        name="run_states",
    )(key_input, value_input, rate)


def gated_kernel(gate_ref, key_ref, value_ref, rate_ref, residue_ref, runs_ref, before_ref, out_ref, signal, conv):
    poles, chans = rate_ref.shape
    steps = key_ref.shape[0] // SUB
    fill_signal(key_ref, value_ref, signal)
    run = lax.broadcasted_iota(jnp.int32, (SUB, LANES), 0)
    run_f = run.astype(f32)
    for tile in range(chans // LANES):
        lanes = pl.ds(tile * LANES, LANES)
        decays, weights, starts = [], [], []
        for r in range(poles):
            rate = jnp.broadcast_to(rate_ref[pl.ds(r, 1), lanes], (SUB, LANES))
            residue = jnp.broadcast_to(residue_ref[pl.ds(r, 1), lanes], (SUB, LANES))
            before = jnp.broadcast_to(before_ref[pl.ds(r, 1), lanes], (SUB, LANES))
            ends = runs_ref[r, :, lanes]
            for back in (1, 2, 4):
                moved = jnp.where(run >= back, pltpu.roll(ends, back, 0), 0.0)
                ends = ends + jnp.exp(-rate * (steps * back)) * moved
            start = jnp.where(run >= 1, pltpu.roll(ends, 1, 0), 0.0)
            starts.append(start + jnp.exp(-rate * (steps * run_f)) * before)
            decays.append(jnp.exp(-rate))
            weights.append(residue * jnp.sqrt(rate))

        def step(j, states):
            at = pl.ds(j, SUB, stride=steps)
            x = signal[tile, at, :]
            states = tuple(d * s + x for d, s in zip(decays, states))
            terms = [w * s for w, s in zip(weights, states)]
            while len(terms) > 1:
                terms = [a + b for a, b in zip(terms[::2], terms[1::2])]
            conv[tile, at, :] = terms[0]
            return states

        lax.fori_loop(0, steps, step, tuple(starts), unroll=4)
    rows = 32
    for part in range(gate_ref.shape[0] // rows):
        at = pl.ds(part * rows, rows)
        for tile in range(chans // LANES):
            lanes = pl.ds(tile * LANES, LANES)
            piece = (gate_ref[at, lanes].astype(f32) * conv[tile, at, :]).astype(bf16)
            for copy in range(NX):
                out_ref[copy, part % NC, pl.ds(part // NC * rows, rows), lanes] = piece


def gated_rows(gate_input, key_input, value_input, rate, residue, runs, before):
    length, chans = gate_input.shape
    return pl.pallas_call(
        gated_kernel,
        out_shape=jax.ShapeDtypeStruct((NX, NC, length // NC, chans), bf16),
        scratch_shapes=[pltpu.VMEM((chans // LANES, length, LANES), f32)] * 2,
        compiler_params=pltpu.CompilerParams(vmem_limit_bytes=32 << 20),
        name="gated_rows",
    )(gate_input, key_input, value_input, rate, residue, runs, before)


def swap(array, axis):
    return lax.ppermute(array, axis, [(0, 1), (1, 0)])


def exchange(array, axes):
    return lax.all_to_all(array, axes, 0, 0, tiled=True)


def copies(array, count):
    return jnp.broadcast_to(array[None], (count, *array.shape))


def state_before(block, rate, length):
    x, h, y = (lax.axis_index(axis) for axis in SEQ)
    blocks = exchange(copies(block, NY), "y")
    at = jnp.arange(NY)[:, None, None]
    back = y - 1 - at
    inner = jnp.sum(
        jnp.where(back >= 0, jnp.exp(-rate * (length * jnp.maximum(back, 0)).astype(f32)), 0.0) * blocks, axis=0
    )
    total = jnp.sum(jnp.exp(-rate * (length * (NY - 1 - at)).astype(f32)) * blocks, axis=0)
    totals = exchange(copies(total, NX * NH), ("x", "h"))
    back = x * NH + h - 1 - jnp.arange(NX * NH)[:, None, None]
    outer = jnp.sum(
        jnp.where(back >= 0, jnp.exp(-rate * (length * NY * jnp.maximum(back, 0)).astype(f32)), 0.0) * totals, axis=0
    )
    return inner + jnp.exp(-rate * (length * y).astype(f32)) * outer


def weight_columns(out_weight):
    h = lax.axis_index("h")
    mine = out_weight.T
    other = swap(mine, "h")
    pair = jnp.where(h == 0, jnp.stack([mine, other]), jnp.stack([other, mine]))
    gathered = lax.all_gather(pair, "y", axis=0, tiled=False)
    own = gathered.transpose(1, 0, 2, 3).reshape(-1, mine.shape[1])
    return own, swap(own, "c")


def body(gate_input, key_input, value_input, decay_rate, residues, out_weight):
    length, chans = gate_input.shape
    rate, residue = decay_rate.T, residues.T
    own_weight, other_weight = weight_columns(out_weight)
    runs, block = run_states(key_input, value_input, rate)
    before = state_before(block, rate, length)
    rows = gated_rows(gate_input, key_input, value_input, rate, residue, runs, before)
    arrived = exchange(rows.reshape(NX * NC, length // NC, chans), ("x", "c"))
    arrived = arrived.reshape(NX, NC, length // NC, chans)
    core = lax.axis_index("c")
    own = lax.dynamic_index_in_dim(arrived, core, 1, keepdims=False).reshape(-1, chans)
    other = lax.dynamic_index_in_dim(arrived, 1 - core, 1, keepdims=False).reshape(-1, chans)
    contract = (((1,), (1,)), ((), ()))
    partial = lax.dot_general(own, own_weight, contract, preferred_element_type=f32) + lax.dot_general(
        other, other_weight, contract, preferred_element_type=f32
    )
    columns = partial.shape[1]
    parts = exchange(partial.astype(bf16).reshape(NX * NZ, -1, columns), ("x", "z"))
    mixed = parts.reshape(NX, NZ, -1, columns).astype(f32).sum(axis=1).astype(bf16)
    return mixed.transpose(1, 0, 2).reshape(-1, NX * columns)


def solution(mesh):
    names, sizes = zip(*AXES)
    fine = Mesh(mesh.devices.reshape(sizes), names)
    return jax.shard_map(
        body,
        mesh=fine,
        in_specs=(P(SEQ, CH), P(SEQ, CH), P(SEQ, CH), P(CH, None), P(CH, None), P(CH, SEQ)),
        out_specs=P(SEQ + CH, None),
        check_vma=False,
    )
```

```python
import jax
import jax.numpy as jnp
from jax import lax
from jax.experimental import pallas as pl
from jax.experimental.pallas import tpu as pltpu
from jax.sharding import Mesh, PartitionSpec as P

AXES = (("x", 4), ("h", 2), ("y", 8), ("z", 4), ("c", 2))
NX, NH, NY, NZ, NC = (size for _, size in AXES)
SEQ = ("x", "h", "y")
CH = ("z", "c")
RING = (1, -1, 2)

SUB = 8
LANES = 128
f32 = jnp.float32
bf16 = jnp.bfloat16


def run_states_kernel(key_ref, value_ref, rate_ref, runs_ref, block_ref, signal):
    poles = rate_ref.shape[0]
    steps = key_ref.shape[0] // SUB
    signal[...] = key_ref[...].astype(f32) * value_ref[...].astype(f32)
    later = (SUB - 1 - lax.broadcasted_iota(jnp.int32, (SUB, LANES), 0)).astype(f32) * steps
    rates = [jnp.broadcast_to(rate_ref[pl.ds(r, 1), :], (SUB, LANES)) for r in range(poles)]
    decays = [jnp.exp(-rate) for rate in rates]

    def step(j, states):
        x = signal[pl.ds(j, SUB, stride=steps), :]
        return tuple(d * s + x for d, s in zip(decays, states))

    states = lax.fori_loop(0, steps, step, (jnp.zeros((SUB, LANES), f32),) * poles, unroll=4)
    ends = []
    for r in range(poles):
        runs_ref[r] = states[r]
        ends.append(jnp.sum(states[r] * jnp.exp(-rates[r] * later), axis=0, keepdims=True))
    ends = jnp.concatenate(ends, axis=0).astype(block_ref.dtype)
    for copy in range(block_ref.shape[0]):
        block_ref[copy] = ends


def run_states(key_input, value_input, rate):
    poles, chans = rate.shape
    length = key_input.shape[0]
    return pl.pallas_call(
        run_states_kernel,
        grid=(chans // LANES,),
        in_specs=[
            pl.BlockSpec((length, LANES), lambda i: (0, i)),
            pl.BlockSpec((length, LANES), lambda i: (0, i)),
            pl.BlockSpec((poles, LANES), lambda i: (0, i)),
        ],
        out_specs=(
            pl.BlockSpec((poles, SUB, LANES), lambda i: (0, 0, i)),
            pl.BlockSpec((NY, poles, LANES), lambda i: (0, 0, i)),
        ),
        out_shape=(
            jax.ShapeDtypeStruct((poles, SUB, chans), f32),
            jax.ShapeDtypeStruct((NY, poles, chans), bf16),
        ),
        scratch_shapes=[pltpu.VMEM((length, LANES), f32)],
        compiler_params=pltpu.CompilerParams(vmem_limit_bytes=60 << 20),
        name="run_states",
    )(key_input, value_input, rate)


def gated_kernel(gate_ref, key_ref, value_ref, rate_ref, residue_ref, runs_ref, before_ref, out_ref, signal, conv):
    poles, chans = rate_ref.shape
    steps = key_ref.shape[0] // SUB
    for tile in range(chans // LANES):
        lanes = pl.ds(tile * LANES, LANES)
        signal[tile] = key_ref[:, lanes].astype(f32) * value_ref[:, lanes].astype(f32)
    run = lax.broadcasted_iota(jnp.int32, (SUB, LANES), 0)
    run_f = run.astype(f32)
    for tile in range(chans // LANES):
        lanes = pl.ds(tile * LANES, LANES)
        decays, weights, starts = [], [], []
        for r in range(poles):
            rate = jnp.broadcast_to(rate_ref[pl.ds(r, 1), lanes], (SUB, LANES))
            residue = jnp.broadcast_to(residue_ref[pl.ds(r, 1), lanes], (SUB, LANES))
            before = jnp.broadcast_to(before_ref[pl.ds(r, 1), lanes], (SUB, LANES))
            ends = runs_ref[r, :, lanes]
            for back in (1, 2, 4):
                moved = jnp.where(run >= back, pltpu.roll(ends, back, 0), 0.0)
                ends = ends + jnp.exp(-rate * (steps * back)) * moved
            start = jnp.where(run >= 1, pltpu.roll(ends, 1, 0), 0.0)
            starts.append(start + jnp.exp(-rate * (steps * run_f)) * before)
            decays.append(jnp.exp(-rate))
            weights.append(residue * jnp.sqrt(rate))

        def step(j, states):
            at = pl.ds(j, SUB, stride=steps)
            x = signal[tile, at, :]
            states = tuple(d * s + x for d, s in zip(decays, states))
            terms = [w * s for w, s in zip(weights, states)]
            while len(terms) > 1:
                terms = [a + b for a, b in zip(terms[::2], terms[1::2])]
            conv[tile, at, :] = terms[0]
            return states

        lax.fori_loop(0, steps, step, tuple(starts), unroll=4)
    rows = gate_ref.shape[0] // (NZ * NC)
    for part in range(NZ * NC):
        at = pl.ds(part * rows, rows)
        for tile in range(chans // LANES):
            lanes = pl.ds(tile * LANES, LANES)
            piece = (gate_ref[at, lanes].astype(f32) * conv[tile, at, :]).astype(bf16)
            for copy in range(NX):
                out_ref[part % NC, copy, pl.ds(part // NC * rows, rows), lanes] = piece


def gated_rows(gate_input, key_input, value_input, rate, residue, runs, before):
    length, chans = gate_input.shape
    return pl.pallas_call(
        gated_kernel,
        out_shape=jax.ShapeDtypeStruct((NC, NX, length // NC, chans), bf16),
        scratch_shapes=[pltpu.VMEM((chans // LANES, length, LANES), f32)] * 2,
        compiler_params=pltpu.CompilerParams(vmem_limit_bytes=32 << 20),
        name="gated_rows",
    )(gate_input, key_input, value_input, rate, residue, runs, before)


def project_kernel(order_ref, rows_ref, own_low, own_high, other_low, other_high, out_ref, own, other):
    core = order_ref[0]
    blocks = order_ref.shape[0] - 1
    half = blocks // 2
    width = own_low.shape[0] // half
    for p in range(blocks):
        at = pl.ds(pl.multiple_of(order_ref[1 + p] * width, width), width)
        of = pl.ds(p % half * width, width)
        own[at, :] = (own_low if p < half else own_high)[of, :]
        other[at, :] = (other_low if p < half else other_high)[of, :]
    contract = (((1,), (1,)), ((), ()))
    total = lax.dot_general(rows_ref[core], own[...], contract, preferred_element_type=f32)
    total += lax.dot_general(rows_ref[1 - core], other[...], contract, preferred_element_type=f32)
    out_ref[...] = total.astype(out_ref.dtype)


def project(order, rows, *weights):
    columns, chans = 2 * weights[0].shape[0], weights[0].shape[1]
    return pl.pallas_call(
        project_kernel,
        in_specs=[pl.BlockSpec(memory_space=pltpu.SMEM)] + [pl.BlockSpec(memory_space=pltpu.VMEM)] * 5,
        out_specs=pl.BlockSpec(memory_space=pltpu.VMEM),
        out_shape=jax.ShapeDtypeStruct((rows.shape[1], columns), bf16),
        scratch_shapes=[pltpu.VMEM((columns, chans), bf16)] * 2,
        compiler_params=pltpu.CompilerParams(vmem_limit_bytes=32 << 20),
        name="project",
    )(order, rows, *weights)


def finish_kernel(parts_ref, out_ref):
    columns = parts_ref.shape[-1]
    for x in range(NX):
        total = parts_ref[x, 0].astype(f32)
        for z in range(1, NZ):
            total += parts_ref[x, z].astype(f32)
        out_ref[:, pl.ds(x * columns, columns)] = total.astype(out_ref.dtype)


def finish(parts):
    return pl.pallas_call(
        finish_kernel,
        out_shape=jax.ShapeDtypeStruct((parts.shape[2], NX * parts.shape[3]), bf16),
        compiler_params=pltpu.CompilerParams(vmem_limit_bytes=32 << 20),
        name="finish",
    )(parts)


def swap(array, axis, bit=1):
    return lax.ppermute(array, axis, [(i, i ^ bit) for i in range(dict(AXES)[axis])])


def from_along_y(array, step):
    return lax.ppermute(array, "y", [((i + step) % NY, i) for i in range(NY)])


def with_other(mine, other):
    return jnp.concatenate([mine, other], axis=0)


def exchange(array, axes):
    return lax.all_to_all(array, axes, 0, 0, tiled=True)


def copies(array, count):
    return jnp.broadcast_to(array[None], (count, *array.shape))


def body(gate_input, key_input, value_input, decay_rate, residues, out_weight):
    length, chans = gate_input.shape
    x, h, y, _, core = (lax.axis_index(axis) for axis, _ in AXES)
    rate, residue = decay_rate.T, residues.T

    weight = out_weight.T
    other = swap(weight, "y", 4)

    runs, block = run_states(key_input, value_input, rate)
    other, block = lax.optimization_barrier((other, block))
    weight = with_other(weight, other)
    other = swap(weight, "h", 1)

    blocks = exchange(block, "y")
    blocks = blocks.astype(f32)
    at = jnp.arange(NY)[:, None, None]
    back = y - 1 - at
    inner = jnp.sum(
        jnp.where(back >= 0, jnp.exp(-rate * (length * jnp.maximum(back, 0)).astype(f32)), 0.0) * blocks, axis=0
    )
    total = jnp.sum(jnp.exp(-rate * (length * (NY - 1 - at)).astype(f32)) * blocks, axis=0)
    weight = with_other(weight, other)
    others = tuple(from_along_y(weight, step) for step in RING)
    totals = exchange(copies(total.astype(bf16), NX * NH), ("x", "h"))
    totals = totals.astype(f32)
    back = x * NH + h - 1 - jnp.arange(NX * NH)[:, None, None]
    outer = jnp.sum(
        jnp.where(back >= 0, jnp.exp(-rate * (length * NY * jnp.maximum(back, 0)).astype(f32)), 0.0) * totals, axis=0
    )
    before = inner + jnp.exp(-rate * (length * y).astype(f32)) * outer

    rows = gated_rows(gate_input, key_input, value_input, rate, residue, runs, before)
    arrived = exchange(rows.reshape(NC * NX, length // NC, chans), ("c", "x")).reshape(NC, -1, chans)
    low, high = with_other(weight, others[0]), with_other(others[1], others[2])
    weights = (low, high, swap(low, "c", 1), swap(high, "c", 1))

    steps, a, b = jnp.array((0, *RING))[:, None, None], jnp.arange(2), jnp.arange(2)[:, None]
    place = ((h ^ b) * NY + ((y + steps) % NY ^ (4 * a))).reshape(-1)
    order = jnp.concatenate([core[None], place]).astype(jnp.int32)
    partial = project(order, arrived, *weights)
    columns = partial.shape[1]
    parts = exchange(partial.reshape(NX * NZ, -1, columns), ("x", "z"))
    return finish(parts.reshape(NX, NZ, -1, columns))


def solution(mesh):
    names, sizes = zip(*AXES)
    fine = Mesh(mesh.devices.reshape(sizes), names)
    return jax.shard_map(
        body,
        mesh=fine,
        in_specs=(P(SEQ, CH), P(SEQ, CH), P(SEQ, CH), P(CH, None), P(CH, None), P(CH, SEQ)),
        out_specs=P(SEQ + CH, None),
        check_vma=False,
    )
```

```python
import jax
import jax.numpy as jnp
from jax import lax
from jax.experimental import pallas as pl
from jax.experimental.pallas import tpu as pltpu
from jax.sharding import Mesh, PartitionSpec as P

AXES = (("x", 4), ("h", 2), ("y", 8), ("z", 4), ("c", 2))
NX, NH, NY, NZ, NC = (size for _, size in AXES)
SEQ = ("x", "h", "y")
CH = ("z", "c")
RING = (2, 1, -1)

SUB = 8
LANES = 128
f32 = jnp.float32
bf16 = jnp.bfloat16


def run_states_kernel(key_ref, value_ref, rate_ref, residue_ref, runs_ref, block_ref, weight_ref, signal):
    weight_ref[...] = residue_ref[...] * jnp.sqrt(rate_ref[...])
    poles, chans = rate_ref.shape
    steps = key_ref.shape[0] // SUB
    later = (SUB - 1 - lax.broadcasted_iota(jnp.int32, (SUB, LANES), 0)).astype(f32) * steps
    for tile in range(chans // LANES):
        lanes = pl.ds(tile * LANES, LANES)
        signal[...] = key_ref[:, lanes].astype(f32) * value_ref[:, lanes].astype(f32)
        rates = [jnp.broadcast_to(rate_ref[pl.ds(r, 1), lanes], (SUB, LANES)) for r in range(poles)]
        decays = [jnp.exp(-rate) for rate in rates]

        def step(j, states):
            x = signal[pl.ds(j, SUB, stride=steps), :]
            return tuple(d * s + x for d, s in zip(decays, states))

        states = lax.fori_loop(0, steps, step, (jnp.zeros((SUB, LANES), f32),) * poles, unroll=8)
        ends = []
        for r in range(poles):
            runs_ref[r, :, lanes] = states[r]
            ends.append(jnp.sum(states[r] * jnp.exp(-rates[r] * later), axis=0, keepdims=True))
        ends = jnp.concatenate(ends, axis=0).astype(block_ref.dtype)
        for copy in range(block_ref.shape[0]):
            block_ref[copy, :, lanes] = ends


def run_states(key_input, value_input, rate, residue):
    poles, chans = rate.shape
    return pl.pallas_call(
        run_states_kernel,
        out_shape=(
            jax.ShapeDtypeStruct((poles, SUB, chans), f32),
            jax.ShapeDtypeStruct((NY, poles, chans), bf16),
            jax.ShapeDtypeStruct((poles, chans), f32),
        ),
        scratch_shapes=[pltpu.VMEM((key_input.shape[0], LANES), f32)],
        compiler_params=pltpu.CompilerParams(vmem_limit_bytes=60 << 20),
        name="run_states",
    )(key_input, value_input, rate, residue)


def gated_kernel(gate_ref, key_ref, value_ref, rate_ref, weight_ref, runs_ref, before_ref, out_ref, signal, conv):
    poles, chans = rate_ref.shape
    steps = key_ref.shape[0] // SUB
    for tile in range(chans // LANES):
        lanes = pl.ds(tile * LANES, LANES)
        signal[tile] = key_ref[:, lanes].astype(f32) * value_ref[:, lanes].astype(f32)
    run = lax.broadcasted_iota(jnp.int32, (SUB, LANES), 0)
    run_f = run.astype(f32)
    for tile in range(chans // LANES):
        lanes = pl.ds(tile * LANES, LANES)
        decays, weights, starts = [], [], []
        for r in range(poles):
            rate = jnp.broadcast_to(rate_ref[pl.ds(r, 1), lanes], (SUB, LANES))
            before = jnp.broadcast_to(before_ref[pl.ds(r, 1), lanes], (SUB, LANES))
            ends = runs_ref[r, :, lanes]
            for back in (1, 2, 4):
                moved = jnp.where(run >= back, pltpu.roll(ends, back, 0), 0.0)
                ends = ends + jnp.exp(-rate * (steps * back)) * moved
            start = jnp.where(run >= 1, pltpu.roll(ends, 1, 0), 0.0)
            starts.append(start + jnp.exp(-rate * (steps * run_f)) * before)
            decays.append(jnp.exp(-rate))
            weights.append(jnp.broadcast_to(weight_ref[pl.ds(r, 1), lanes], (SUB, LANES)))

        def step(j, states):
            at = pl.ds(j, SUB, stride=steps)
            x = signal[tile, at, :]
            states = tuple(d * s + x for d, s in zip(decays, states))
            terms = [w * s for w, s in zip(weights, states)]
            while len(terms) > 1:
                terms = [a + b for a, b in zip(terms[::2], terms[1::2])]
            conv[tile, at, :] = terms[0]
            return states

        lax.fori_loop(0, steps, step, tuple(starts), unroll=True)
    rows = gate_ref.shape[0] // (NZ * NC)
    for part in range(NZ * NC):
        at = pl.ds(part * rows, rows)
        for tile in range(chans // LANES):
            lanes = pl.ds(tile * LANES, LANES)
            piece = (gate_ref[at, lanes].astype(f32) * conv[tile, at, :]).astype(bf16)
            for copy in range(NX):
                out_ref[part % NC, copy, pl.ds(part // NC * rows, rows), lanes] = piece


def gated_rows(gate_input, key_input, value_input, rate, pole_weight, runs, before):
    length, chans = gate_input.shape
    return pl.pallas_call(
        gated_kernel,
        out_shape=jax.ShapeDtypeStruct((NC, NX, length // NC, chans), bf16),
        scratch_shapes=[pltpu.VMEM((chans // LANES, length, LANES), f32)] * 2,
        compiler_params=pltpu.CompilerParams(vmem_limit_bytes=32 << 20),
        name="gated_rows",
    )(gate_input, key_input, value_input, rate, pole_weight, runs, before)


def project_kernel(place_ref, rows_ref, own_low, own_high, other_low, other_high, out_ref, own, other):
    h, y, core = place_ref[0], place_ref[1], place_ref[2]
    blocks = NH * NY
    half = blocks // 2
    width = own_low.shape[0] // half
    for p in range(blocks):
        step, b, a = (0, *RING)[p // 4], p // 2 % 2, p % 2
        block = (h + b) % NH * NY + (y + step + 4 * a + NY) % NY
        at = pl.ds(pl.multiple_of(block * width, width), width)
        of = pl.ds(p % half * width, width)
        own[at, :] = (own_low if p < half else own_high)[of, :]
        other[at, :] = (other_low if p < half else other_high)[of, :]
    contract = (((1,), (1,)), ((), ()))
    total = lax.dot_general(rows_ref[core], own[...], contract, preferred_element_type=f32)
    total += lax.dot_general(rows_ref[1 - core], other[...], contract, preferred_element_type=f32)
    rows = out_ref.shape[2]
    for x in range(NX):
        for z in range(NZ):
            out_ref[z, x] = total[(x * NZ + z) * rows : (x * NZ + z + 1) * rows].astype(out_ref.dtype)


def project(place, rows, *weights):
    columns, chans = 2 * weights[0].shape[0], weights[0].shape[1]
    return pl.pallas_call(
        project_kernel,
        in_specs=[pl.BlockSpec(memory_space=pltpu.SMEM)] + [pl.BlockSpec(memory_space=pltpu.VMEM)] * 5,
        out_specs=pl.BlockSpec(memory_space=pltpu.VMEM),
        out_shape=jax.ShapeDtypeStruct((NZ, NX, rows.shape[1] // (NZ * NX), columns), bf16),
        scratch_shapes=[pltpu.VMEM((columns, chans), bf16)] * 2,
        compiler_params=pltpu.CompilerParams(vmem_limit_bytes=32 << 20),
        name="project",
    )(place, rows, *weights)


def finish_kernel(parts_ref, out_ref):
    columns = parts_ref.shape[-1]
    for x in range(NX):
        total = parts_ref[0, x].astype(f32)
        for z in range(1, NZ):
            total += parts_ref[z, x].astype(f32)
        out_ref[:, pl.ds(x * columns, columns)] = total.astype(out_ref.dtype)


def finish(parts):
    return pl.pallas_call(
        finish_kernel,
        out_shape=jax.ShapeDtypeStruct((parts.shape[2], NX * parts.shape[3]), bf16),
        compiler_params=pltpu.CompilerParams(vmem_limit_bytes=32 << 20),
        name="finish",
    )(parts)


def swap(array, axis, bit=1):
    return lax.ppermute(array, axis, [(i, i ^ bit) for i in range(dict(AXES)[axis])])


def from_along_y(array, step):
    return lax.ppermute(array, "y", [((i + step) % NY, i) for i in range(NY)])


def with_other(mine, other):
    return jnp.concatenate([mine, other], axis=0)


def exchange(array, axes):
    return lax.all_to_all(array, axes, 0, 0, tiled=True)


def copies(array, count):
    return jnp.broadcast_to(array[None], (count, *array.shape))


def body(gate_input, key_input, value_input, decay_rate, residues, out_weight):
    length, chans = gate_input.shape
    x, h, y, _, core = (lax.axis_index(axis) for axis, _ in AXES)
    rate, residue = decay_rate.T, residues.T

    weight = out_weight.T
    other = swap(weight, "y", 4)

    runs, block, pole_weight = run_states(key_input, value_input, rate, residue)
    weight = with_other(weight, other)
    other = swap(weight, "h", 1)

    blocks = exchange(block, "y")
    blocks = blocks.astype(f32)
    at = jnp.arange(NY)[:, None, None]
    back = y - 1 - at
    inner = jnp.sum(
        jnp.where(back >= 0, jnp.exp(-rate * (length * jnp.maximum(back, 0)).astype(f32)), 0.0) * blocks, axis=0
    )
    total = jnp.sum(jnp.exp(-rate * (length * (NY - 1 - at)).astype(f32)) * blocks, axis=0)
    weight = with_other(weight, other)
    others = [from_along_y(weight, step) for step in RING[:2]]
    totals = exchange(copies(total.astype(bf16), NX * NH), ("x", "h"))
    totals = totals.astype(f32)
    back = x * NH + h - 1 - jnp.arange(NX * NH)[:, None, None]
    outer = jnp.sum(
        jnp.where(back >= 0, jnp.exp(-rate * (length * NY * jnp.maximum(back, 0)).astype(f32)), 0.0) * totals, axis=0
    )
    before = inner + jnp.exp(-rate * (length * y).astype(f32)) * outer

    rows = gated_rows(gate_input, key_input, value_input, rate, pole_weight, runs, before)
    late, rows = lax.optimization_barrier((weight, rows))
    others.append(from_along_y(late, RING[2]))
    arrived = exchange(rows.reshape(NC * NX, length // NC, chans), ("c", "x")).reshape(NC, -1, chans)
    low, high = with_other(weight, others[0]), with_other(others[1], others[2])
    weights = (low, high, swap(low, "c", 1), swap(high, "c", 1))

    place = jnp.stack([h, y, core]).astype(jnp.int32)
    partial = project(place, arrived, *weights)
    columns = partial.shape[-1]
    parts = exchange(partial.reshape(NZ * NX, -1, columns), ("z", "x"))
    return finish(parts.reshape(NZ, NX, -1, columns))


def solution(mesh):
    names, sizes = zip(*AXES)
    fine = Mesh(mesh.devices.reshape(sizes), names)
    return jax.shard_map(
        body,
        mesh=fine,
        in_specs=(P(SEQ, CH), P(SEQ, CH), P(SEQ, CH), P(CH, None), P(CH, None), P(CH, SEQ)),
        out_specs=P(SEQ + CH, None),
        check_vma=False,
    )
```

```python
import jax
import jax.numpy as jnp
from jax import lax
from jax.experimental import pallas as pl
from jax.experimental.pallas import tpu as pltpu
from jax.sharding import Mesh, PartitionSpec as P

AXES = (("x", 4), ("h", 2), ("y", 8), ("z", 4), ("c", 2))
NX, NH, NY, NZ, NC = (size for _, size in AXES)
SEQ = ("x", "h", "y")
CH = ("z", "c")
RING = (2, 1, -1)

SUB = 8
LANES = 128
f32 = jnp.float32
bf16 = jnp.bfloat16


def run_states_kernel(key_ref, value_ref, rate_ref, residue_ref, runs_ref, block_ref, signal):
    poles, chans = rate_ref.shape
    for r in range(0, poles, SUB):
        at = pl.ds(r, SUB)
        runs_ref[poles + r // SUB] = residue_ref[at, :] * jnp.sqrt(rate_ref[at, :])
    steps = key_ref.shape[0] // SUB
    later = (SUB - 1 - lax.broadcasted_iota(jnp.int32, (SUB, LANES), 0)).astype(f32) * steps
    for tile in range(chans // LANES):
        lanes = pl.ds(tile * LANES, LANES)
        signal[...] = key_ref[:, lanes].astype(f32) * value_ref[:, lanes].astype(f32)
        rates = [jnp.broadcast_to(rate_ref[pl.ds(r, 1), lanes], (SUB, LANES)) for r in range(poles)]
        decays = [jnp.exp(-rate) for rate in rates]

        def step(j, states):
            x = signal[pl.ds(j, SUB, stride=steps), :]
            return tuple(d * s + x for d, s in zip(decays, states))

        states = lax.fori_loop(0, steps, step, (jnp.zeros((SUB, LANES), f32),) * poles, unroll=8)
        ends = []
        for r in range(poles):
            runs_ref[r, :, lanes] = states[r]
            ends.append(jnp.sum(states[r] * jnp.exp(-rates[r] * later), axis=0, keepdims=True))
        ends = jnp.concatenate(ends, axis=0).astype(block_ref.dtype)
        for copy in range(block_ref.shape[0]):
            block_ref[copy, :, lanes] = ends


def run_states(key_input, value_input, rate, residue):
    poles, chans = rate.shape
    return pl.pallas_call(
        run_states_kernel,
        out_shape=(
            jax.ShapeDtypeStruct((poles + poles // SUB, SUB, chans), f32),
            jax.ShapeDtypeStruct((NY, poles, chans), bf16),
        ),
        scratch_shapes=[pltpu.VMEM((key_input.shape[0], LANES), f32)],
        compiler_params=pltpu.CompilerParams(vmem_limit_bytes=60 << 20),
        name="run_states",
    )(key_input, value_input, rate, residue)


def gated_kernel(gate_ref, key_ref, value_ref, rate_ref, runs_ref, before_ref, out_ref, signal, conv):
    poles, chans = rate_ref.shape
    steps = key_ref.shape[0] // SUB
    for tile in range(chans // LANES):
        lanes = pl.ds(tile * LANES, LANES)
        signal[tile] = key_ref[:, lanes].astype(f32) * value_ref[:, lanes].astype(f32)
    run = lax.broadcasted_iota(jnp.int32, (SUB, LANES), 0)
    run_f = run.astype(f32)
    for tile in range(chans // LANES):
        lanes = pl.ds(tile * LANES, LANES)
        decays, weights, starts = [], [], []
        for r in range(poles):
            rate = jnp.broadcast_to(rate_ref[pl.ds(r, 1), lanes], (SUB, LANES))
            before = jnp.broadcast_to(before_ref[pl.ds(r, 1), lanes], (SUB, LANES))
            ends = runs_ref[r, :, lanes]
            for back in (1, 2, 4):
                moved = jnp.where(run >= back, pltpu.roll(ends, back, 0), 0.0)
                ends = ends + jnp.exp(-rate * (steps * back)) * moved
            start = jnp.where(run >= 1, pltpu.roll(ends, 1, 0), 0.0)
            starts.append(start + jnp.exp(-rate * (steps * run_f)) * before)
            decays.append(jnp.exp(-rate))
            weight = runs_ref[poles + r // SUB, pl.ds(r % SUB, 1), lanes]
            weights.append(jnp.broadcast_to(weight, (SUB, LANES)))

        def step(j, states):
            at = pl.ds(j, SUB, stride=steps)
            x = signal[tile, at, :]
            states = tuple(d * s + x for d, s in zip(decays, states))
            terms = [w * s for w, s in zip(weights, states)]
            while len(terms) > 1:
                terms = [a + b for a, b in zip(terms[::2], terms[1::2])]
            conv[tile, at, :] = terms[0]
            return states

        lax.fori_loop(0, steps, step, tuple(starts), unroll=True)
    rows = gate_ref.shape[0] // (NZ * NC)
    for part in range(NZ * NC):
        at = pl.ds(part * rows, rows)
        for tile in range(chans // LANES):
            lanes = pl.ds(tile * LANES, LANES)
            piece = (gate_ref[at, lanes].astype(f32) * conv[tile, at, :]).astype(bf16)
            for copy in range(NX):
                out_ref[part % NC, copy, pl.ds(part // NC * rows, rows), lanes] = piece


def gated_rows(gate_input, key_input, value_input, rate, runs, before):
    length, chans = gate_input.shape
    return pl.pallas_call(
        gated_kernel,
        out_shape=jax.ShapeDtypeStruct((NC, NX, length // NC, chans), bf16),
        scratch_shapes=[pltpu.VMEM((chans // LANES, length, LANES), f32)] * 2,
        compiler_params=pltpu.CompilerParams(vmem_limit_bytes=32 << 20),
        name="gated_rows",
    )(gate_input, key_input, value_input, rate, runs, before)


def project_kernel(place_ref, rows_ref, own_low, own_high, other_low, other_high, out_ref, own, other):
    h, y, core = place_ref[0], place_ref[1], place_ref[2]
    blocks = NH * NY
    half = blocks // 2
    width = own_low.shape[0] // half
    for p in range(blocks):
        step, a, b = (0, *RING)[p // 4], p // 2 % 2, p % 2
        block = (h + b) % NH * NY + (y + step + 4 * a + NY) % NY
        at = pl.ds(pl.multiple_of(block * width, width), width)
        of = pl.ds(p % half * width, width)
        own[at, :] = (own_low if p < half else own_high)[of, :]
        other[at, :] = (other_low if p < half else other_high)[of, :]
    contract = (((1,), (1,)), ((), ()))
    total = lax.dot_general(rows_ref[core], own[...], contract, preferred_element_type=f32)
    total += lax.dot_general(rows_ref[1 - core], other[...], contract, preferred_element_type=f32)
    rows = out_ref.shape[2]
    for x in range(NX):
        for z in range(NZ):
            out_ref[z, x] = total[(x * NZ + z) * rows : (x * NZ + z + 1) * rows].astype(out_ref.dtype)


def project(place, rows, *weights):
    columns, chans = 2 * weights[0].shape[0], weights[0].shape[1]
    return pl.pallas_call(
        project_kernel,
        in_specs=[pl.BlockSpec(memory_space=pltpu.SMEM)] + [pl.BlockSpec(memory_space=pltpu.VMEM)] * 5,
        out_specs=pl.BlockSpec(memory_space=pltpu.VMEM),
        out_shape=jax.ShapeDtypeStruct((NZ, NX, rows.shape[1] // (NZ * NX), columns), bf16),
        scratch_shapes=[pltpu.VMEM((columns, chans), bf16)] * 2,
        compiler_params=pltpu.CompilerParams(vmem_limit_bytes=32 << 20),
        name="project",
    )(place, rows, *weights)


def finish_kernel(parts_ref, out_ref):
    columns = parts_ref.shape[-1]
    for x in range(NX):
        total = parts_ref[0, x].astype(f32)
        for z in range(1, NZ):
            total += parts_ref[z, x].astype(f32)
        out_ref[:, pl.ds(x * columns, columns)] = total.astype(out_ref.dtype)


def finish(parts):
    return pl.pallas_call(
        finish_kernel,
        out_shape=jax.ShapeDtypeStruct((parts.shape[2], NX * parts.shape[3]), bf16),
        compiler_params=pltpu.CompilerParams(vmem_limit_bytes=32 << 20),
        name="finish",
    )(parts)


def swap(array, axis, bit=1):
    return lax.ppermute(array, axis, [(i, i ^ bit) for i in range(dict(AXES)[axis])])


def from_along_y(array, step):
    return lax.ppermute(array, "y", [((i + step) % NY, i) for i in range(NY)])


def with_other(mine, other):
    return jnp.concatenate([mine, other], axis=0)


def exchange(array, axes):
    return lax.all_to_all(array, axes, 0, 0, tiled=True)


def copies(array, count):
    return jnp.broadcast_to(array[None], (count, *array.shape))


def body(gate_input, key_input, value_input, decay_rate, residues, out_weight):
    length, chans = gate_input.shape
    x, h, y, _, core = (lax.axis_index(axis) for axis, _ in AXES)
    rate, residue = decay_rate.T, residues.T

    weight = out_weight.T
    other = swap(weight, "h", 1)

    runs, block = run_states(key_input, value_input, rate, residue)
    weight = with_other(weight, other)
    other = swap(weight, "y", 4)

    blocks = exchange(block, "y")
    blocks = blocks.astype(f32)
    at = jnp.arange(NY)[:, None, None]
    back = y - 1 - at
    inner = jnp.sum(
        jnp.where(back >= 0, jnp.exp(-rate * (length * jnp.maximum(back, 0)).astype(f32)), 0.0) * blocks, axis=0
    )
    total = jnp.sum(jnp.exp(-rate * (length * (NY - 1 - at)).astype(f32)) * blocks, axis=0)
    weight = with_other(weight, other)
    others = [from_along_y(weight, step) for step in RING[:2]]
    totals = exchange(copies(total.astype(bf16), NX * NH), ("x", "h"))
    totals = totals.astype(f32)
    back = x * NH + h - 1 - jnp.arange(NX * NH)[:, None, None]
    outer = jnp.sum(
        jnp.where(back >= 0, jnp.exp(-rate * (length * NY * jnp.maximum(back, 0)).astype(f32)), 0.0) * totals, axis=0
    )
    before = inner + jnp.exp(-rate * (length * y).astype(f32)) * outer

    rows = gated_rows(gate_input, key_input, value_input, rate, runs, before)
    late, rows = lax.optimization_barrier((weight, rows))
    others.append(from_along_y(late, RING[2]))
    arrived = exchange(rows.reshape(NC * NX, length // NC, chans), ("c", "x")).reshape(NC, -1, chans)
    low, high = with_other(weight, others[0]), with_other(others[1], others[2])
    weights = (low, high, swap(low, "c", 1), swap(high, "c", 1))

    place = jnp.stack([h, y, core]).astype(jnp.int32)
    partial = project(place, arrived, *weights)
    columns = partial.shape[-1]
    parts = exchange(partial.reshape(NZ * NX, -1, columns), ("z", "x"))
    return finish(parts.reshape(NZ, NX, -1, columns))


def solution(mesh):
    names, sizes = zip(*AXES)
    fine = Mesh(mesh.devices.reshape(sizes), names)
    return jax.shard_map(
        body,
        mesh=fine,
        in_specs=(P(SEQ, CH), P(SEQ, CH), P(SEQ, CH), P(CH, None), P(CH, None), P(CH, SEQ)),
        out_specs=P(SEQ + CH, None),
        check_vma=False,
    )
```

```python
import jax
import jax.numpy as jnp
from jax import lax
from jax.experimental import pallas as pl
from jax.experimental.pallas import tpu as pltpu
from jax.sharding import Mesh, PartitionSpec as P

AXES = (("x", 4), ("h", 2), ("y", 8), ("z", 4), ("c", 2))
NX, NH, NY, NZ, NC = (size for _, size in AXES)
SEQ = ("x", "h", "y")
CH = ("z", "c")
RING = (2, -1, 1)

SUB = 8
LANES = 128
f32 = jnp.float32
bf16 = jnp.bfloat16


def run_states_kernel(key_ref, value_ref, rate_ref, residue_ref, runs_ref, block_ref, signal):
    poles, chans = rate_ref.shape
    for r in range(0, poles, SUB):
        at = pl.ds(r, SUB)
        runs_ref[poles + r // SUB] = residue_ref[at, :] * jnp.sqrt(rate_ref[at, :])
    steps = key_ref.shape[0] // SUB
    later = (SUB - 1 - lax.broadcasted_iota(jnp.int32, (SUB, LANES), 0)).astype(f32) * steps
    for tile in range(chans // LANES):
        lanes = pl.ds(tile * LANES, LANES)
        signal[...] = key_ref[:, lanes].astype(f32) * value_ref[:, lanes].astype(f32)
        rates = [jnp.broadcast_to(rate_ref[pl.ds(r, 1), lanes], (SUB, LANES)) for r in range(poles)]
        decays = [jnp.exp(-rate) for rate in rates]

        def step(j, states):
            x = signal[pl.ds(j, SUB, stride=steps), :]
            return tuple(d * s + x for d, s in zip(decays, states))

        states = lax.fori_loop(0, steps, step, (jnp.zeros((SUB, LANES), f32),) * poles, unroll=8)
        ends = []
        for r in range(poles):
            runs_ref[r, :, lanes] = states[r]
            ends.append(jnp.sum(states[r] * jnp.exp(-rates[r] * later), axis=0, keepdims=True))
        ends = jnp.concatenate(ends, axis=0).astype(block_ref.dtype)
        for copy in range(block_ref.shape[0]):
            block_ref[copy, :, lanes] = ends


def run_states(key_input, value_input, rate, residue):
    poles, chans = rate.shape
    return pl.pallas_call(
        run_states_kernel,
        out_shape=(
            jax.ShapeDtypeStruct((poles + poles // SUB, SUB, chans), f32),
            jax.ShapeDtypeStruct((NY, poles, chans), bf16),
        ),
        scratch_shapes=[pltpu.VMEM((key_input.shape[0], LANES), f32)],
        compiler_params=pltpu.CompilerParams(vmem_limit_bytes=60 << 20),
        name="run_states",
    )(key_input, value_input, rate, residue)


def gated_kernel(gate_ref, key_ref, value_ref, rate_ref, runs_ref, before_ref, out_ref, signal, conv):
    poles, chans = rate_ref.shape
    steps = key_ref.shape[0] // SUB
    for tile in range(chans // LANES):
        lanes = pl.ds(tile * LANES, LANES)
        signal[tile] = key_ref[:, lanes].astype(f32) * value_ref[:, lanes].astype(f32)
    run = lax.broadcasted_iota(jnp.int32, (SUB, LANES), 0)
    run_f = run.astype(f32)
    for tile in range(chans // LANES):
        lanes = pl.ds(tile * LANES, LANES)
        decays, weights, starts = [], [], []
        for r in range(poles):
            rate = jnp.broadcast_to(rate_ref[pl.ds(r, 1), lanes], (SUB, LANES))
            before = jnp.broadcast_to(before_ref[pl.ds(r, 1), lanes], (SUB, LANES))
            ends = runs_ref[r, :, lanes]
            for back in (1, 2, 4):
                moved = jnp.where(run >= back, pltpu.roll(ends, back, 0), 0.0)
                ends = ends + jnp.exp(-rate * (steps * back)) * moved
            start = jnp.where(run >= 1, pltpu.roll(ends, 1, 0), 0.0)
            starts.append(start + jnp.exp(-rate * (steps * run_f)) * before)
            decays.append(jnp.exp(-rate))
            weight = runs_ref[poles + r // SUB, pl.ds(r % SUB, 1), lanes]
            weights.append(jnp.broadcast_to(weight, (SUB, LANES)))

        def step(j, states):
            at = pl.ds(j, SUB, stride=steps)
            x = signal[tile, at, :]
            states = tuple(d * s + x for d, s in zip(decays, states))
            terms = [w * s for w, s in zip(weights, states)]
            while len(terms) > 1:
                terms = [a + b for a, b in zip(terms[::2], terms[1::2])]
            conv[tile, at, :] = terms[0]
            return states

        lax.fori_loop(0, steps, step, tuple(starts), unroll=True)
    rows = gate_ref.shape[0] // (NZ * NC)
    for part in range(NZ * NC):
        at = pl.ds(part * rows, rows)
        for tile in range(chans // LANES):
            lanes = pl.ds(tile * LANES, LANES)
            piece = (gate_ref[at, lanes].astype(f32) * conv[tile, at, :]).astype(bf16)
            for copy in range(NX):
                out_ref[part % NC, copy, pl.ds(part // NC * rows, rows), lanes] = piece


def gated_rows(gate_input, key_input, value_input, rate, runs, before):
    length, chans = gate_input.shape
    return pl.pallas_call(
        gated_kernel,
        out_shape=jax.ShapeDtypeStruct((NC, NX, length // NC, chans), bf16),
        scratch_shapes=[pltpu.VMEM((chans // LANES, length, LANES), f32)] * 2,
        compiler_params=pltpu.CompilerParams(vmem_limit_bytes=32 << 20),
        name="gated_rows",
    )(gate_input, key_input, value_input, rate, runs, before)


def project_kernel(place_ref, rows_ref, own_low, own_high, other_low, other_high, out_ref, own, other):
    h, y, core = place_ref[0], place_ref[1], place_ref[2]
    blocks = NH * NY
    half = blocks // 2
    width = own_low.shape[0] // half
    for p in range(blocks):
        step, a, b = (0, *RING)[p // 4], p // 2 % 2, p % 2
        block = (h + b) % NH * NY + (y + step + 4 * a + NY) % NY
        at = pl.ds(pl.multiple_of(block * width, width), width)
        of = pl.ds(p % half * width, width)
        own[at, :] = (own_low if p < half else own_high)[of, :]
        other[at, :] = (other_low if p < half else other_high)[of, :]
    contract = (((1,), (1,)), ((), ()))
    total = lax.dot_general(rows_ref[core], own[...], contract, preferred_element_type=f32)
    total += lax.dot_general(rows_ref[1 - core], other[...], contract, preferred_element_type=f32)
    rows = out_ref.shape[2]
    for x in range(NX):
        for z in range(NZ):
            out_ref[z, x] = total[(x * NZ + z) * rows : (x * NZ + z + 1) * rows].astype(out_ref.dtype)


def project(place, rows, *weights):
    columns, chans = 2 * weights[0].shape[0], weights[0].shape[1]
    return pl.pallas_call(
        project_kernel,
        in_specs=[pl.BlockSpec(memory_space=pltpu.SMEM)] + [pl.BlockSpec(memory_space=pltpu.VMEM)] * 5,
        out_specs=pl.BlockSpec(memory_space=pltpu.VMEM),
        out_shape=jax.ShapeDtypeStruct((NZ, NX, rows.shape[1] // (NZ * NX), columns), bf16),
        scratch_shapes=[pltpu.VMEM((columns, chans), bf16)] * 2,
        compiler_params=pltpu.CompilerParams(vmem_limit_bytes=32 << 20),
        name="project",
    )(place, rows, *weights)


def finish_kernel(parts_ref, out_ref):
    columns = parts_ref.shape[-1]
    for x in range(NX):
        total = parts_ref[0, x].astype(f32)
        for z in range(1, NZ):
            total += parts_ref[z, x].astype(f32)
        out_ref[:, pl.ds(x * columns, columns)] = total.astype(out_ref.dtype)


def finish(parts):
    return pl.pallas_call(
        finish_kernel,
        out_shape=jax.ShapeDtypeStruct((parts.shape[2], NX * parts.shape[3]), bf16),
        compiler_params=pltpu.CompilerParams(vmem_limit_bytes=32 << 20),
        name="finish",
    )(parts)


def swap(array, axis, bit=1):
    return lax.ppermute(array, axis, [(i, i ^ bit) for i in range(dict(AXES)[axis])])


def from_along_y(array, step):
    return lax.ppermute(array, "y", [((i + step) % NY, i) for i in range(NY)])


def with_other(mine, other):
    return jnp.concatenate([mine, other], axis=0)


def exchange(array, axes):
    return lax.all_to_all(array, axes, 0, 0, tiled=True)


def copies(array, count):
    return jnp.broadcast_to(array[None], (count, *array.shape))


def body(gate_input, key_input, value_input, decay_rate, residues, out_weight):
    length, chans = gate_input.shape
    x, h, y, _, core = (lax.axis_index(axis) for axis, _ in AXES)
    rate, residue = decay_rate.T, residues.T

    weight = out_weight.T
    other = swap(weight, "h", 1)

    runs, block = run_states(key_input, value_input, rate, residue)
    weight = with_other(weight, other)
    other = swap(weight, "y", 4)

    blocks = exchange(block, "y")
    blocks = blocks.astype(f32)
    at = jnp.arange(NY)[:, None, None]
    back = y - 1 - at
    inner = jnp.sum(
        jnp.where(back >= 0, jnp.exp(-rate * (length * jnp.maximum(back, 0)).astype(f32)), 0.0) * blocks, axis=0
    )
    total = jnp.sum(jnp.exp(-rate * (length * (NY - 1 - at)).astype(f32)) * blocks, axis=0)
    weight = with_other(weight, other)
    others = [from_along_y(weight, step) for step in RING[:2]]
    totals = exchange(copies(total.astype(bf16), NX * NH), ("x", "h"))
    totals = totals.astype(f32)
    back = x * NH + h - 1 - jnp.arange(NX * NH)[:, None, None]
    outer = jnp.sum(
        jnp.where(back >= 0, jnp.exp(-rate * (length * NY * jnp.maximum(back, 0)).astype(f32)), 0.0) * totals, axis=0
    )
    before = inner + jnp.exp(-rate * (length * y).astype(f32)) * outer

    rows = gated_rows(gate_input, key_input, value_input, rate, runs, before)
    late, rows = lax.optimization_barrier((weight, rows))
    others.append(from_along_y(late, RING[2]))
    arrived = exchange(rows.reshape(NC * NX, length // NC, chans), ("c", "x")).reshape(NC, -1, chans)
    low, high = with_other(weight, others[0]), with_other(others[1], others[2])
    weights = (low, high, swap(low, "c", 1), swap(high, "c", 1))

    place = jnp.stack([h, y, core]).astype(jnp.int32)
    partial = project(place, arrived, *weights)
    columns = partial.shape[-1]
    parts = exchange(partial.reshape(NZ * NX, -1, columns), ("z", "x"))
    return finish(parts.reshape(NZ, NX, -1, columns))


def solution(mesh):
    names, sizes = zip(*AXES)
    fine = Mesh(mesh.devices.reshape(sizes), names)
    return jax.shard_map(
        body,
        mesh=fine,
        in_specs=(P(SEQ, CH), P(SEQ, CH), P(SEQ, CH), P(CH, None), P(CH, None), P(CH, SEQ)),
        out_specs=P(SEQ + CH, None),
        check_vma=False,
    )
```

```python
import jax
import jax.numpy as jnp
from jax import lax
from jax.experimental import pallas as pl
from jax.experimental.pallas import tpu as pltpu
from jax.sharding import Mesh, PartitionSpec as P

AXES = (("x", 4), ("h", 2), ("y", 8), ("z", 4), ("c", 2))
NX, NH, NY, NZ, NC = (size for _, size in AXES)
SEQ = ("x", "h", "y")
CH = ("z", "c")
RING = (2, -1, 1)

SUB = 8
LANES = 128
f32 = jnp.float32
bf16 = jnp.bfloat16


def run_states_kernel(key_ref, value_ref, rate_ref, residue_ref, runs_ref, block_ref, signal):
    poles, chans = rate_ref.shape
    for r in range(0, poles, SUB):
        at = pl.ds(r, SUB)
        runs_ref[poles + r // SUB] = residue_ref[at, :] * jnp.sqrt(rate_ref[at, :])
    steps = key_ref.shape[0] // SUB
    later = SUB - 1 - lax.broadcasted_iota(jnp.int32, (SUB, LANES), 0)
    for tile in range(chans // LANES):
        lanes = pl.ds(tile * LANES, LANES)
        signal[...] = key_ref[:, lanes].astype(f32) * value_ref[:, lanes].astype(f32)
        rates = [jnp.broadcast_to(rate_ref[pl.ds(r, 1), lanes], (SUB, LANES)) for r in range(poles)]
        decays = [jnp.exp(-rate) for rate in rates]

        def step(j, states):
            x = signal[pl.ds(j, SUB, stride=steps), :]
            return tuple(d * s + x for d, s in zip(decays, states))

        states = lax.fori_loop(0, steps, step, (jnp.zeros((SUB, LANES), f32),) * poles, unroll=True)
        ends = []
        for r in range(poles):
            runs_ref[r, :, lanes] = states[r]
            fade, faded = jnp.exp(-rates[r] * steps), states[r]
            for runs in (1, 2, 4):
                faded = jnp.where(later // runs % 2 == 1, fade * faded, faded)
                fade = fade * fade
            ends.append(jnp.sum(faded, axis=0, keepdims=True))
        ends = jnp.concatenate(ends, axis=0).astype(block_ref.dtype)
        for copy in range(block_ref.shape[0]):
            block_ref[copy, :, lanes] = ends


def run_states(key_input, value_input, rate, residue):
    poles, chans = rate.shape
    return pl.pallas_call(
        run_states_kernel,
        out_shape=(
            jax.ShapeDtypeStruct((poles + poles // SUB, SUB, chans), f32),
            jax.ShapeDtypeStruct((NY, poles, chans), bf16),
        ),
        scratch_shapes=[pltpu.VMEM((key_input.shape[0], LANES), f32)],
        compiler_params=pltpu.CompilerParams(vmem_limit_bytes=60 << 20),
        name="run_states",
    )(key_input, value_input, rate, residue)


def gated_kernel(gate_ref, key_ref, value_ref, rate_ref, runs_ref, before_ref, out_ref, signal, conv):
    poles, chans = rate_ref.shape
    steps = key_ref.shape[0] // SUB
    for tile in range(chans // LANES):
        lanes = pl.ds(tile * LANES, LANES)
        signal[tile] = key_ref[:, lanes].astype(f32) * value_ref[:, lanes].astype(f32)
    run = lax.broadcasted_iota(jnp.int32, (SUB, LANES), 0)
    run_f = run.astype(f32)
    for tile in range(chans // LANES):
        lanes = pl.ds(tile * LANES, LANES)
        decays, weights, starts = [], [], []
        for r in range(poles):
            rate = jnp.broadcast_to(rate_ref[pl.ds(r, 1), lanes], (SUB, LANES))
            before = jnp.broadcast_to(before_ref[pl.ds(r, 1), lanes], (SUB, LANES))
            ends = runs_ref[r, :, lanes]
            for back in (1, 2, 4):
                moved = jnp.where(run >= back, pltpu.roll(ends, back, 0), 0.0)
                ends = ends + jnp.exp(-rate * (steps * back)) * moved
            start = jnp.where(run >= 1, pltpu.roll(ends, 1, 0), 0.0)
            starts.append(start + jnp.exp(-rate * (steps * run_f)) * before)
            decays.append(jnp.exp(-rate))
            weight = runs_ref[poles + r // SUB, pl.ds(r % SUB, 1), lanes]
            weights.append(jnp.broadcast_to(weight, (SUB, LANES)))

        def step(j, states):
            at = pl.ds(j, SUB, stride=steps)
            x = signal[tile, at, :]
            states = tuple(d * s + x for d, s in zip(decays, states))
            terms = [w * s for w, s in zip(weights, states)]
            while len(terms) > 1:
                terms = [a + b for a, b in zip(terms[::2], terms[1::2])]
            conv[tile, at, :] = terms[0]
            return states

        lax.fori_loop(0, steps, step, tuple(starts), unroll=True)
    rows = gate_ref.shape[0] // (NZ * NC)
    for part in range(NZ * NC):
        at = pl.ds(part * rows, rows)
        for tile in range(chans // LANES):
            lanes = pl.ds(tile * LANES, LANES)
            piece = (gate_ref[at, lanes].astype(f32) * conv[tile, at, :]).astype(bf16)
            for copy in range(NX):
                out_ref[part % NC, copy, pl.ds(part // NC * rows, rows), lanes] = piece


def gated_rows(gate_input, key_input, value_input, rate, runs, before):
    length, chans = gate_input.shape
    return pl.pallas_call(
        gated_kernel,
        out_shape=jax.ShapeDtypeStruct((NC, NX, length // NC, chans), bf16),
        scratch_shapes=[pltpu.VMEM((chans // LANES, length, LANES), f32)] * 2,
        compiler_params=pltpu.CompilerParams(vmem_limit_bytes=32 << 20),
        name="gated_rows",
    )(gate_input, key_input, value_input, rate, runs, before)


def project_kernel(place_ref, rows_ref, own_low, own_high, other_low, other_high, out_ref, own, other):
    h, y, core = place_ref[0], place_ref[1], place_ref[2]
    blocks = NH * NY
    half = blocks // 2
    width = own_low.shape[0] // half
    for p in range(blocks):
        step, a, b = (0, *RING)[p // 4], p // 2 % 2, p % 2
        block = (h + b) % NH * NY + (y + step + 4 * a + NY) % NY
        at = pl.ds(pl.multiple_of(block * width, width), width)
        of = pl.ds(p % half * width, width)
        own[at, :] = (own_low if p < half else own_high)[of, :]
        other[at, :] = (other_low if p < half else other_high)[of, :]
    contract = (((1,), (1,)), ((), ()))
    total = lax.dot_general(rows_ref[core], own[...], contract, preferred_element_type=f32)
    total += lax.dot_general(rows_ref[1 - core], other[...], contract, preferred_element_type=f32)
    rows = out_ref.shape[2]
    for x in range(NX):
        for z in range(NZ):
            out_ref[z, x] = total[(x * NZ + z) * rows : (x * NZ + z + 1) * rows].astype(out_ref.dtype)


def project(place, rows, *weights):
    columns, chans = 2 * weights[0].shape[0], weights[0].shape[1]
    return pl.pallas_call(
        project_kernel,
        in_specs=[pl.BlockSpec(memory_space=pltpu.SMEM)] + [pl.BlockSpec(memory_space=pltpu.VMEM)] * 5,
        out_specs=pl.BlockSpec(memory_space=pltpu.VMEM),
        out_shape=jax.ShapeDtypeStruct((NZ, NX, rows.shape[1] // (NZ * NX), columns), bf16),
        scratch_shapes=[pltpu.VMEM((columns, chans), bf16)] * 2,
        compiler_params=pltpu.CompilerParams(vmem_limit_bytes=32 << 20),
        name="project",
    )(place, rows, *weights)


def finish_kernel(parts_ref, out_ref):
    columns = parts_ref.shape[-1]
    for x in range(NX):
        total = parts_ref[0, x].astype(f32)
        for z in range(1, NZ):
            total += parts_ref[z, x].astype(f32)
        out_ref[:, pl.ds(x * columns, columns)] = total.astype(out_ref.dtype)


def finish(parts):
    return pl.pallas_call(
        finish_kernel,
        out_shape=jax.ShapeDtypeStruct((parts.shape[2], NX * parts.shape[3]), bf16),
        compiler_params=pltpu.CompilerParams(vmem_limit_bytes=32 << 20),
        name="finish",
    )(parts)


def swap(array, axis, bit=1):
    return lax.ppermute(array, axis, [(i, i ^ bit) for i in range(dict(AXES)[axis])])


def from_along_y(array, step):
    return lax.ppermute(array, "y", [((i + step) % NY, i) for i in range(NY)])


def with_other(mine, other):
    return jnp.concatenate([mine, other], axis=0)


def exchange(array, axes):
    return lax.all_to_all(array, axes, 0, 0, tiled=True)


def copies(array, count):
    return jnp.broadcast_to(array[None], (count, *array.shape))


def body(gate_input, key_input, value_input, decay_rate, residues, out_weight):
    length, chans = gate_input.shape
    x, h, y, _, core = (lax.axis_index(axis) for axis, _ in AXES)
    rate, residue = decay_rate.T, residues.T

    weight = out_weight.T
    other = swap(weight, "h", 1)

    runs, block = run_states(key_input, value_input, rate, residue)
    weight = with_other(weight, other)
    other = swap(weight, "y", 4)

    blocks = exchange(block, "y")
    blocks = blocks.astype(f32)
    at = jnp.arange(NY)[:, None, None]
    back = y - 1 - at
    inner = jnp.sum(
        jnp.where(back >= 0, jnp.exp(-rate * (length * jnp.maximum(back, 0)).astype(f32)), 0.0) * blocks, axis=0
    )
    total = jnp.sum(jnp.exp(-rate * (length * (NY - 1 - at)).astype(f32)) * blocks, axis=0)
    weight = with_other(weight, other)
    others = [from_along_y(weight, step) for step in RING[:2]]
    totals = exchange(copies(total.astype(bf16), NX * NH), ("x", "h"))
    totals = totals.astype(f32)
    back = x * NH + h - 1 - jnp.arange(NX * NH)[:, None, None]
    outer = jnp.sum(
        jnp.where(back >= 0, jnp.exp(-rate * (length * NY * jnp.maximum(back, 0)).astype(f32)), 0.0) * totals, axis=0
    )
    before = inner + jnp.exp(-rate * (length * y).astype(f32)) * outer

    rows = gated_rows(gate_input, key_input, value_input, rate, runs, before)
    late, rows = lax.optimization_barrier((weight, rows))
    others.append(from_along_y(late, RING[2]))
    arrived = exchange(rows.reshape(NC * NX, length // NC, chans), ("c", "x")).reshape(NC, -1, chans)
    low, high = with_other(weight, others[0]), with_other(others[1], others[2])
    weights = (low, high, swap(low, "c", 1), swap(high, "c", 1))

    place = jnp.stack([h, y, core]).astype(jnp.int32)
    partial = project(place, arrived, *weights)
    columns = partial.shape[-1]
    parts = exchange(partial.reshape(NZ * NX, -1, columns), ("z", "x"))
    return finish(parts.reshape(NZ, NX, -1, columns))


def solution(mesh):
    names, sizes = zip(*AXES)
    fine = Mesh(mesh.devices.reshape(sizes), names)
    return jax.shard_map(
        body,
        mesh=fine,
        in_specs=(P(SEQ, CH), P(SEQ, CH), P(SEQ, CH), P(CH, None), P(CH, None), P(CH, SEQ)),
        out_specs=P(SEQ + CH, None),
        check_vma=False,
    )
```

```python
import jax
import jax.numpy as jnp
from jax import lax
from jax.experimental import pallas as pl
from jax.experimental.pallas import tpu as pltpu
from jax.sharding import Mesh, PartitionSpec as P

AXES = (("x", 4), ("h", 2), ("y", 8), ("z", 4), ("c", 2))
NX, NH, NY, NZ, NC = (size for _, size in AXES)
SEQ = ("x", "h", "y")
CH = ("z", "c")
RING = (-2, -1, 1)

SUB = 8
LANES = 128
f32 = jnp.float32
bf16 = jnp.bfloat16


def run_states_kernel(key_ref, value_ref, rate_ref, residue_ref, runs_ref, block_ref, signal):
    poles, chans = rate_ref.shape
    for r in range(0, poles, SUB):
        at = pl.ds(r, SUB)
        runs_ref[poles + r // SUB] = residue_ref[at, :] * jnp.sqrt(rate_ref[at, :])
    steps = key_ref.shape[0] // SUB
    later = (SUB - 1 - lax.broadcasted_iota(jnp.int32, (SUB, LANES), 0)).astype(f32) * steps
    for tile in range(chans // LANES):
        lanes = pl.ds(tile * LANES, LANES)
        signal[...] = key_ref[:, lanes].astype(f32) * value_ref[:, lanes].astype(f32)
        rates = [jnp.broadcast_to(rate_ref[pl.ds(r, 1), lanes], (SUB, LANES)) for r in range(poles)]
        decays = [jnp.exp(-rate) for rate in rates]

        def step(j, states):
            x = signal[pl.ds(j, SUB, stride=steps), :]
            return tuple(d * s + x for d, s in zip(decays, states))

        states = lax.fori_loop(0, steps, step, (jnp.zeros((SUB, LANES), f32),) * poles, unroll=8)
        ends = []
        for r in range(poles):
            runs_ref[r, :, lanes] = states[r]
            ends.append(jnp.sum(states[r] * jnp.exp(-rates[r] * later), axis=0, keepdims=True))
        ends = jnp.concatenate(ends, axis=0).astype(block_ref.dtype)
        for copy in range(block_ref.shape[0]):
            block_ref[copy, :, lanes] = ends


def run_states(key_input, value_input, rate, residue):
    poles, chans = rate.shape
    return pl.pallas_call(
        run_states_kernel,
        out_shape=(
            jax.ShapeDtypeStruct((poles + poles // SUB, SUB, chans), f32),
            jax.ShapeDtypeStruct((NY, poles, chans), bf16),
        ),
        scratch_shapes=[pltpu.VMEM((key_input.shape[0], LANES), f32)],
        compiler_params=pltpu.CompilerParams(vmem_limit_bytes=60 << 20),
        name="run_states",
    )(key_input, value_input, rate, residue)


def gated_kernel(gate_ref, key_ref, value_ref, rate_ref, runs_ref, before_ref, out_ref, signal, conv):
    poles, chans = rate_ref.shape
    steps = key_ref.shape[0] // SUB
    for tile in range(chans // LANES):
        lanes = pl.ds(tile * LANES, LANES)
        signal[tile] = key_ref[:, lanes].astype(f32) * value_ref[:, lanes].astype(f32)
    run = lax.broadcasted_iota(jnp.int32, (SUB, LANES), 0)
    run_f = run.astype(f32)
    for tile in range(chans // LANES):
        lanes = pl.ds(tile * LANES, LANES)
        decays, weights, starts = [], [], []
        for r in range(poles):
            rate = jnp.broadcast_to(rate_ref[pl.ds(r, 1), lanes], (SUB, LANES))
            before = jnp.broadcast_to(before_ref[pl.ds(r, 1), lanes], (SUB, LANES))
            ends = runs_ref[r, :, lanes]
            for back in (1, 2, 4):
                moved = jnp.where(run >= back, pltpu.roll(ends, back, 0), 0.0)
                ends = ends + jnp.exp(-rate * (steps * back)) * moved
            start = jnp.where(run >= 1, pltpu.roll(ends, 1, 0), 0.0)
            starts.append(start + jnp.exp(-rate * (steps * run_f)) * before)
            decays.append(jnp.exp(-rate))
            weight = runs_ref[poles + r // SUB, pl.ds(r % SUB, 1), lanes]
            weights.append(jnp.broadcast_to(weight, (SUB, LANES)))

        def step(j, states):
            at = pl.ds(j, SUB, stride=steps)
            x = signal[tile, at, :]
            states = tuple(d * s + x for d, s in zip(decays, states))
            terms = [w * s for w, s in zip(weights, states)]
            while len(terms) > 1:
                terms = [a + b for a, b in zip(terms[::2], terms[1::2])]
            conv[tile, at, :] = terms[0]
            return states

        lax.fori_loop(0, steps, step, tuple(starts), unroll=True)
    rows = gate_ref.shape[0] // (NZ * NC)
    for part in range(NZ * NC):
        at = pl.ds(part * rows, rows)
        for tile in range(chans // LANES):
            lanes = pl.ds(tile * LANES, LANES)
            piece = (gate_ref[at, lanes].astype(f32) * conv[tile, at, :]).astype(bf16)
            for copy in range(NX):
                out_ref[part % NC, copy, pl.ds(part // NC * rows, rows), lanes] = piece


def gated_rows(gate_input, key_input, value_input, rate, runs, before):
    length, chans = gate_input.shape
    return pl.pallas_call(
        gated_kernel,
        out_shape=jax.ShapeDtypeStruct((NC, NX, length // NC, chans), bf16),
        scratch_shapes=[pltpu.VMEM((chans // LANES, length, LANES), f32)] * 2,
        compiler_params=pltpu.CompilerParams(vmem_limit_bytes=32 << 20),
        name="gated_rows",
    )(gate_input, key_input, value_input, rate, runs, before)


def project_kernel(place_ref, rows_ref, own_low, own_high, other_low, other_high, out_ref, own, other):
    h, y, core = place_ref[0], place_ref[1], place_ref[2]
    blocks = NH * NY
    half = blocks // 2
    width = own_low.shape[0] // half
    for p in range(blocks):
        step, a, b = (0, *RING)[p // 4], p // 2 % 2, p % 2
        block = (h + b) % NH * NY + (y + step + 4 * a + NY) % NY
        at = pl.ds(pl.multiple_of(block * width, width), width)
        of = pl.ds(p % half * width, width)
        own[at, :] = (own_low if p < half else own_high)[of, :]
        other[at, :] = (other_low if p < half else other_high)[of, :]
    contract = (((1,), (1,)), ((), ()))
    total = lax.dot_general(rows_ref[core], own[...], contract, preferred_element_type=f32)
    total += lax.dot_general(rows_ref[1 - core], other[...], contract, preferred_element_type=f32)
    rows = out_ref.shape[2]
    for x in range(NX):
        for z in range(NZ):
            out_ref[z, x] = total[(x * NZ + z) * rows : (x * NZ + z + 1) * rows].astype(out_ref.dtype)


def project(place, rows, *weights):
    columns, chans = 2 * weights[0].shape[0], weights[0].shape[1]
    return pl.pallas_call(
        project_kernel,
        in_specs=[pl.BlockSpec(memory_space=pltpu.SMEM)] + [pl.BlockSpec(memory_space=pltpu.VMEM)] * 5,
        out_specs=pl.BlockSpec(memory_space=pltpu.VMEM),
        out_shape=jax.ShapeDtypeStruct((NZ, NX, rows.shape[1] // (NZ * NX), columns), bf16),
        scratch_shapes=[pltpu.VMEM((columns, chans), bf16)] * 2,
        compiler_params=pltpu.CompilerParams(vmem_limit_bytes=32 << 20),
        name="project",
    )(place, rows, *weights)


def finish_kernel(parts_ref, out_ref):
    columns = parts_ref.shape[-1]
    for x in range(NX):
        total = parts_ref[0, x].astype(f32)
        for z in range(1, NZ):
            total += parts_ref[z, x].astype(f32)
        out_ref[:, pl.ds(x * columns, columns)] = total.astype(out_ref.dtype)


def finish(parts):
    return pl.pallas_call(
        finish_kernel,
        out_shape=jax.ShapeDtypeStruct((parts.shape[2], NX * parts.shape[3]), bf16),
        compiler_params=pltpu.CompilerParams(vmem_limit_bytes=32 << 20),
        name="finish",
    )(parts)


def swap(array, axis, bit=1):
    return lax.ppermute(array, axis, [(i, i ^ bit) for i in range(dict(AXES)[axis])])


def from_along_y(array, step):
    return lax.ppermute(array, "y", [((i + step) % NY, i) for i in range(NY)])


def with_other(mine, other):
    return jnp.concatenate([mine, other], axis=0)


def exchange(array, axes):
    return lax.all_to_all(array, axes, 0, 0, tiled=True)


def copies(array, count):
    return jnp.broadcast_to(array[None], (count, *array.shape))


def body(gate_input, key_input, value_input, decay_rate, residues, out_weight):
    length, chans = gate_input.shape
    x, h, y, _, core = (lax.axis_index(axis) for axis, _ in AXES)
    rate, residue = decay_rate.T, residues.T

    weight = out_weight.T
    other = swap(weight, "h", 1)

    runs, block = run_states(key_input, value_input, rate, residue)
    weight = with_other(weight, other)
    other = swap(weight, "y", 4)

    blocks = exchange(block, "y")
    blocks = blocks.astype(f32)
    at = jnp.arange(NY)[:, None, None]
    back = y - 1 - at
    inner = jnp.sum(
        jnp.where(back >= 0, jnp.exp(-rate * (length * jnp.maximum(back, 0)).astype(f32)), 0.0) * blocks, axis=0
    )
    total = jnp.sum(jnp.exp(-rate * (length * (NY - 1 - at)).astype(f32)) * blocks, axis=0)
    weight = with_other(weight, other)
    others = [from_along_y(weight, step) for step in RING[:2]]
    totals = exchange(copies(total.astype(bf16), NX * NH), ("x", "h"))
    totals = totals.astype(f32)
    back = x * NH + h - 1 - jnp.arange(NX * NH)[:, None, None]
    outer = jnp.sum(
        jnp.where(back >= 0, jnp.exp(-rate * (length * NY * jnp.maximum(back, 0)).astype(f32)), 0.0) * totals, axis=0
    )
    before = inner + jnp.exp(-rate * (length * y).astype(f32)) * outer

    rows = gated_rows(gate_input, key_input, value_input, rate, runs, before)
    late, rows = lax.optimization_barrier((weight, rows))
    others.append(from_along_y(late, RING[2]))
    arrived = exchange(rows.reshape(NC * NX, length // NC, chans), ("c", "x")).reshape(NC, -1, chans)
    low, high = with_other(weight, others[0]), with_other(others[1], others[2])
    weights = (low, high, swap(low, "c", 1), swap(high, "c", 1))

    place = jnp.stack([h, y, core]).astype(jnp.int32)
    partial = project(place, arrived, *weights)
    columns = partial.shape[-1]
    parts = exchange(partial.reshape(NZ * NX, -1, columns), ("z", "x"))
    return finish(parts.reshape(NZ, NX, -1, columns))


def solution(mesh):
    names, sizes = zip(*AXES)
    fine = Mesh(mesh.devices.reshape(sizes), names)
    return jax.shard_map(
        body,
        mesh=fine,
        in_specs=(P(SEQ, CH), P(SEQ, CH), P(SEQ, CH), P(CH, None), P(CH, None), P(CH, SEQ)),
        out_specs=P(SEQ + CH, None),
        check_vma=False,
    )
```
